32 devices in a mesh: groups: 2 (over y), tm: 4 (over z), height: 4 (over x, core).
Axes of the slice: x: 2, y: 2, z: 4, core: 2. Of those that a mesh axis runs over, the one named last changes fastest.
Arguments:
- video: bfloat16 [16, 16, 64, 256], P(('groups', 'tm'), 'height'), parts along dimension 0, may hold values from -8 to 8
- norm_gain: float32 [256], replicated, may hold values from 0.25 to 1.75
- spatial_weight: bfloat16 [3, 3, 256, 256], P(None, None, 'height'), may hold values from -0.125 to 0.125
- temporal_weight: bfloat16 [3, 256, 256], replicated, may hold values from -0.21875 to 0.21875
- haar_weight: bfloat16 [2048, 512], replicated, may hold values from -0.125 to 0.125
- query_weight: bfloat16 [512, 512], replicated, may hold values from -1.5 to 1.5
- key_weight: bfloat16 [512, 512], replicated, may hold values from -1.5 to 1.5
Outputs:
- encoded: bfloat16 [8, 8, 32, 512], P(('groups', 'tm'), 'height'), parts along dimension 0
The draws below stay inside these ranges and needn't reach their ends.
There are 2 independent parts, one for each index of `groups`. The reference program is written for one: setup_inputs(seed, part) draws one part's arguments, and reference() takes and returns one part's arrays. A program takes and returns all parts, laid end to end along the dimension named above; an argument that names none is the same for every part. Nothing has to cross between parts.
All inputs are finite; a program needn't handle non-finite values.
Results may differ from the reference program's by a relative error of at most 0.015.
Values may be sent and summed in bfloat16 or wider, within the bound.
A program may use at most 64 MiB of HBM per device.

```python
import jax
import jax.numpy as jnp
from jax import lax

C = 256
C2 = 512
HEAD_DIM = 64
COLS = 64
FRAMES = 8
ROWS = 16


def draw_video(key, part):
    noise_key = jax.random.fold_in(jax.random.fold_in(key, 11), 0)
    values = jnp.clip(jax.random.normal(noise_key, (FRAMES, ROWS, COLS, C), jnp.float32), -6.0, 6.0)
    return values.astype(jnp.bfloat16)


def attention_pair(key):
    subkeys = jax.random.split(jax.random.fold_in(key, 29), 2)
    spread = C2 ** (-0.5)
    query_own = spread * jax.random.normal(subkeys[0], (C2, C2), jnp.float32)
    key_own = spread * jax.random.normal(subkeys[1], (C2, C2), jnp.float32)
    query_values = jnp.clip(query_own, -6.0 * spread, 6.0 * spread)
    key_values = jnp.clip(key_own, -6.0 * spread, 6.0 * spread)
    return (query_values, key_values)


def draw_query_weight(key, part):
    return attention_pair(key)[0].astype(jnp.bfloat16)


def draw_key_weight(key, part):
    return attention_pair(key)[1].astype(jnp.bfloat16)


def levels(stream_key, shape, cuts, least, high):
    loudness = 1.0
    for dim, blocks in cuts:
        draws = jax.random.uniform(jax.random.fold_in(jax.random.fold_in(stream_key, 6), dim), (blocks,), jnp.float32, least / len(cuts), high / len(cuts))
        loudness = loudness * jnp.repeat(jnp.exp(draws), shape[dim] // blocks).reshape((-1,) + (1,) * (len(shape) - 1 - dim))
    return loudness


def gaussian(rng, dims, scale, limit, cuts=(), held_as=jnp.bfloat16):
    loudness = levels(rng, dims, cuts, -0.22, 0.18) if cuts else 1.0
    values = jax.random.normal(rng, dims, jnp.float32) * scale * loudness
    return jnp.minimum(jnp.maximum(values, -limit), limit).astype(held_as)


def setup_inputs(seed: int = 0, part: int = 0) -> dict:
    key_list = jax.random.split(jax.random.key(seed), 8)
    own_keys = jax.random.split(jax.random.fold_in(key_list[7], part), 8)
    video = draw_video(jax.random.fold_in(jax.random.fold_in(key_list[7], part), 71), part)
    norm_gain = jnp.clip(1.0 + 0.15 * jax.random.normal(key_list[1], (C,), jnp.float32), 0.25, 1.75)
    spatial_weight = gaussian(key_list[2], (3, 3, C, C), (9 * C) ** -0.5, 0.125, ((2, 4),))
    temporal_weight = gaussian(key_list[3], (3, C, C), (3 * C) ** -0.5, 0.21875)
    haar_weight = gaussian(key_list[4], (8 * C, C2), (8 * C) ** -0.5, 0.125)
    query_weight = draw_query_weight(jax.random.fold_in(key_list[7], 71), part)
    key_weight = draw_key_weight(jax.random.fold_in(key_list[7], 71), part)
    return dict(video=video, norm_gain=norm_gain, spatial_weight=spatial_weight, temporal_weight=temporal_weight, haar_weight=haar_weight, query_weight=query_weight, key_weight=key_weight)


epsilon = 1e-06
inv_root = 0.7071067811865476

def activate(video, norm_gain):
    values = video.astype(jnp.float32)
    square = lax.optimization_barrier(jnp.mean(values * values, axis=-1, keepdims=True))
    normed = values * lax.rsqrt(square + epsilon) * norm_gain
    return (normed * jax.nn.sigmoid(normed)).astype(jnp.bfloat16)

def haar_split(values, axis_pos):
    first = lax.index_in_dim(values, 0, axis_pos, keepdims=False)
    second = lax.index_in_dim(values, 1, axis_pos, keepdims=False)
    return jnp.stack([first + second, first - second], axis=axis_pos) * inv_root

def haar_bands(merged):
    frames, rows, columns, channels = merged.shape
    values = merged.astype(jnp.float32).reshape(frames // 2, 2, rows // 2, 2, columns // 2, 2, channels)
    for axis_pos in (1, 3, 5):
        values = haar_split(values, axis_pos)
    values = jnp.transpose(values, (0, 2, 4, 1, 3, 5, 6))
    return values.reshape(frames // 2, rows // 2, columns // 2, 8 * channels).astype(jnp.bfloat16)

def causal_attention(queries, keys, values, head_dim):
    frames, places, width = queries.shape
    heads = width // head_dim
    query_heads = queries.astype(jnp.float32).reshape(frames, places, heads, head_dim)
    key_heads = keys.astype(jnp.float32).reshape(frames, places, heads, head_dim)
    value_heads = values.astype(jnp.float32).reshape(frames, places, heads, head_dim)
    scores = jnp.einsum('tphd,sphd->phts', query_heads, key_heads) * head_dim ** (-0.5)
    order = jnp.arange(frames)
    allowed = order[None, :] <= order[:, None]
    scores = jnp.where(allowed, scores, -1e+30)
    top = lax.optimization_barrier(jnp.max(scores, axis=-1, keepdims=True))
    weights = jnp.exp(scores - top)
    probs = (weights / lax.optimization_barrier(jnp.sum(weights, axis=-1, keepdims=True))).astype(jnp.bfloat16)
    mixed = jnp.einsum('phts,sphd->tphd', probs.astype(jnp.float32), value_heads)
    return mixed.reshape(frames, places, width).astype(jnp.bfloat16)

def reference(video, norm_gain, spatial_weight, temporal_weight, haar_weight, query_weight, key_weight):
    frames, rows, columns, channels = video.shape
    outward = spatial_weight.shape[3]
    acted = activate(video, norm_gain)
    padded = jnp.pad(acted, ((0, 0), (1, 1), (1, 1), (0, 0)))
    total = jnp.zeros((frames * rows * columns, outward), jnp.float32)
    for row_tap in range(3):
        for col_tap in range(3):
            window = padded[:, row_tap:row_tap + rows, col_tap:col_tap + columns, :].reshape(-1, channels)
            total = total + jnp.dot(window, spatial_weight[row_tap, col_tap], preferred_element_type=jnp.float32)
    spatial = total.astype(jnp.bfloat16).reshape(frames, rows, columns, outward)
    extended = jnp.pad(spatial, ((2, 0), (0, 0), (0, 0), (0, 0)))
    temporal = jnp.zeros((frames * rows * columns, channels), jnp.float32)
    for frame_tap in range(3):
        window = extended[frame_tap:frame_tap + frames].reshape(-1, outward)
        temporal = temporal + jnp.dot(window, temporal_weight[frame_tap], preferred_element_type=jnp.float32)
    merged = (video.astype(jnp.float32).reshape(-1, channels) + temporal).astype(jnp.bfloat16)
    bands = haar_bands(merged.reshape(frames, rows, columns, channels))
    coarse_frames, coarse_rows, coarse_cols, band_width = bands.shape
    latent = jnp.dot(bands.reshape(-1, band_width), haar_weight, preferred_element_type=jnp.float32).astype(jnp.bfloat16)
    queries = jnp.dot(latent, query_weight, preferred_element_type=jnp.float32).astype(jnp.bfloat16)
    keys = jnp.dot(latent, key_weight, preferred_element_type=jnp.float32).astype(jnp.bfloat16)
    width = latent.shape[1]
    places = coarse_rows * coarse_cols
    latent_three = latent.reshape(coarse_frames, places, width)
    mixed = causal_attention(queries.reshape(coarse_frames, places, width), keys.reshape(coarse_frames, places, width), latent_three, HEAD_DIM)
    result = (latent_three.astype(jnp.float32) + mixed.astype(jnp.float32)).astype(jnp.bfloat16)
    return result.reshape(coarse_frames, coarse_rows, coarse_cols, width)
```

```python
import functools

import jax
import jax.numpy as jnp
import numpy as np
from jax import lax
from jax.experimental import pallas as pl
from jax.experimental.pallas import tpu as pltpu
from jax.sharding import PartitionSpec as P

HEAD_DIM = 64
epsilon = 1e-06
inv_root = 0.7071067811865476
MESH = pl.DeviceIdType.MESH


def haar_matrix(cols):
    half = cols // 2
    band = np.arange(4 * cols)[:, None] // half
    place = np.arange(4 * cols)[:, None] % half
    item = np.arange(4 * cols)[None, :]
    frame, row, col = item // (2 * cols), (item // cols) % 2, item % cols
    odd = (band // 4) * frame + ((band // 2) % 2) * row + (band % 2) * (col % 2)
    return np.where(col // 2 == place, np.where(odd % 2 == 1, -1.0, 1.0), 0.0)


def kernel(
    nh, nt, video, gain, sw, tw, hw, qw, kw, haar, heads, out,
    vid, wfull, twv, hwv, qwv, kwv, haarv, headsv, patches, acc, sp, mg, bands, gl, sc,
    local_sem, wsend, wrecv, fsend, frecv, hsend, hrecv, gsend, grecv, vsend, vrecv, lsend, lrecv,
):
    h, t = lax.axis_index("height"), lax.axis_index("tm")
    frames, rows, cols, chan = video.shape
    cin = sw.shape[2]
    chips = nh // 2
    chip, core = lax.div(h, 2), lax.rem(h, 2)
    sibling = chip * 2 + 1 - core
    f32, bf16 = jnp.float32, jnp.bfloat16

    def remote(src, dst, send, recv, **where):
        return pltpu.make_async_remote_copy(
            src_ref=src, dst_ref=dst, send_sem=send, recv_sem=recv, device_id=where, device_id_type=MESH
        )

    own_in = pl.ds(pl.multiple_of(h * cin, cin), cin)
    local = [
        pltpu.make_async_copy(video, vid.at[pl.ds(2, frames), pl.ds(1, rows)], local_sem.at[0]),
        pltpu.make_async_copy(sw, wfull.at[:, :, own_in, :], local_sem.at[1]),
        pltpu.make_async_copy(tw, twv, local_sem.at[2]),
        pltpu.make_async_copy(haar, haarv, local_sem.at[3]),
        pltpu.make_async_copy(hw, hwv, local_sem.at[4]),
        pltpu.make_async_copy(qw, qwv, local_sem.at[5]),
        pltpu.make_async_copy(kw, kwv, local_sem.at[6]),
        pltpu.make_async_copy(heads, headsv, local_sem.at[7]),
    ]
    for copy in local:
        copy.start()

    barrier = pltpu.get_barrier_semaphore()
    for d in range(1, nh):
        pl.semaphore_signal(barrier, inc=1, device_id={"height": lax.rem(h + d, nh)}, device_id_type=MESH)
    for d in range(1, nt):
        pl.semaphore_signal(barrier, inc=1, device_id={"tm": lax.rem(t + d, nt)}, device_id_type=MESH)

    total = frames + 2
    for edge, slot in ((0, 0), (nh - 1, rows + 1)):
        @pl.when(h == edge)
        def _():
            vid[:, slot] = jnp.zeros((total, cols, chan), bf16)

    @pl.when(t == 0)
    def _():
        for f in range(2):
            vid[f] = jnp.zeros((rows + 2, cols, chan), bf16)

    for d in range(1, nt):
        @pl.when(t < d)
        def _():
            gl[d] = jnp.zeros(gl.shape[1:], bf16)

    pl.semaphore_wait(barrier, nh - 1 + nt - 1)

    later = {"tm": lax.rem(t + 1, nt)}
    above, below = {"height": lax.rem(h + nh - 1, nh)}, {"height": lax.rem(h + 1, nh)}
    tail = video.at[pl.ds(frames - 2, 2)]
    mine = pl.ds(2, frames)
    halo = [
        remote(video.at[:, 0], vid.at[mine, rows + 1], hsend.at[0], hrecv.at[0], **above),
        remote(video.at[:, rows - 1], vid.at[mine, 0], hsend.at[1], hrecv.at[1], **below),
    ]
    past = [
        remote(tail.at[:, 0], vid.at[pl.ds(0, 2), 1], vsend.at[0], vrecv.at[0], **later),
        remote(tail.at[:, rows - 1], vid.at[pl.ds(0, 2), rows], vsend.at[1], vrecv.at[1], **later),
        remote(
            tail.at[:, pl.ds(1, rows - 2)], vid.at[pl.ds(0, 2), pl.ds(2, rows - 2)],
            vsend.at[2], vrecv.at[2], **later,
        ),
    ]
    relay = [
        remote(vid.at[pl.ds(0, 2), 1], vid.at[pl.ds(0, 2), rows + 1], gsend.at[0], grecv.at[0], **above),
        remote(vid.at[pl.ds(0, 2), rows], vid.at[pl.ds(0, 2), 0], gsend.at[1], grecv.at[1], **below),
    ]
    up, down, has_past, has_next = h > 0, h < nh - 1, t > 0, t < nt - 1
    sends = (up, down)
    receives = (down, up)

    weights, onward = {}, {}
    for a in range(3):
        piece = wfull.at[a, :, own_in, :]
        weights[0, a] = remote(
            sw.at[a], piece, wsend.at[0, a], wrecv.at[0, a], height=sibling
        )
        for d in range(1, chips):
            weights[d, a] = remote(
                sw.at[a], piece, wsend.at[d, a], wrecv.at[d, a],
                height=lax.rem(chip + d, chips) * 2 + core,
            )
            origin = lax.rem(chip + chips - d, chips) * 2 + core
            held = wfull.at[a, :, pl.ds(pl.multiple_of(origin * cin, cin), cin), :]
            onward[d, a] = remote(held, held, fsend.at[d, a], frecv.at[d, a], height=sibling)

    for cond, copy in zip(sends, halo):
        pl.when(cond)(copy.start)
    for copy in past:
        pl.when(has_next)(copy.start)
    for a in range(3):
        for d in range(1, chips):
            weights[d, a].start()
        weights[0, a].start()

    column = lax.broadcasted_iota(jnp.int32, (cols, chan), 0)
    scale = gain[...]

    def activate(f, r):
        values = vid[f, r].astype(f32)
        square = jnp.mean(values * values, axis=-1, keepdims=True)
        normed = values * lax.rsqrt(square + epsilon) * scale
        acted = normed * jax.nn.sigmoid(normed)
        before = jnp.where(column == 0, 0.0, pltpu.roll(acted, 1, 0))
        after = jnp.where(column == cols - 1, 0.0, pltpu.roll(acted, cols - 1, 0))
        patches[f, r, :, pl.ds(0, chan)] = before.astype(bf16)
        patches[f, r, :, pl.ds(chan, chan)] = acted.astype(bf16)
        patches[f, r, :, pl.ds(2 * chan, chan)] = after.astype(bf16)

    def activate_rows(first, count, row, height):
        def step(i, carry):
            activate(first + lax.div(i, height), row + lax.rem(i, height))
            return carry
        lax.fori_loop(0, count * height, step, 0)

    def receive(copies):
        for copy in copies:
            copy.wait_recv()

    local[0].wait()
    activate_rows(2, frames, 1, rows)
    for i in range(2):
        pl.when(has_past)(past[i].wait_recv)
        pl.when(has_past & sends[i])(relay[i].start)
    for i, row in ((0, rows + 1), (1, 0)):
        pl.when(receives[i])(halo[i].wait_recv)
        activate_rows(2, frames, row, 1)
    for d in range(1, chips):
        weights[d, 0].wait_recv()
        onward[d, 0].start()
    pl.when(has_past)(past[2].wait_recv)
    activate_rows(0, 2, 1, rows)
    for d in range(1, chips):
        weights[d, 1].wait_recv()
        onward[d, 1].start()
    for i, row in ((0, rows + 1), (1, 0)):
        pl.when(has_past & receives[i])(relay[i].wait_recv)
        activate_rows(0, 2, row, 1)
    local[1].wait()
    for a in range(3):
        if a == 1:
            for d in range(1, chips):
                weights[d, 2].wait_recv()
                onward[d, 2].start()
        weights[0, a].wait_recv()
        receive([onward[d, a] for d in range(1, chips)])
        taps = wfull[a].reshape(3 * chan, wfull.shape[3])
        for f in range(total):
            part = jnp.dot(
                patches[f, a : a + rows].reshape(rows * cols, 3 * chan), taps,
                preferred_element_type=f32,
            )
            if a == 0:
                acc[f] = part
            elif a == 1:
                acc[f] += part
            else:
                sp[f] = (acc[f] + part).astype(bf16)

    local[2].wait()
    for f in range(frames):
        temporal = jnp.dot(sp[f], twv[0], preferred_element_type=f32)
        for k in (1, 2):
            temporal += jnp.dot(sp[f + k], twv[k], preferred_element_type=f32)
        own = vid[f + 2, 1 : rows + 1].reshape(rows * cols, chan).astype(f32)
        mg[f] = (own + temporal).astype(bf16)

    local[3].wait()
    half = cols // 2
    for j in range(rows // 2):
        pair = pl.ds(2 * j * cols, 2 * cols)
        block = jnp.concatenate([mg[0, pair], mg[1, pair]], axis=0)
        split = jnp.dot(haarv[...], block, preferred_element_type=f32) * (inv_root * inv_root * inv_root)
        for band in range(8):
            bands[pl.ds(j * half, half), pl.ds(band * chan, chan)] = split[
                band * half : (band + 1) * half
            ].astype(bf16)
    local[4].wait()
    latent = jnp.dot(bands[...], hwv[...], preferred_element_type=f32).astype(bf16)
    gl[0] = latent

    shares = [None]
    for d in range(1, nt):
        shares.append(
            remote(gl.at[0], gl.at[d], lsend.at[d], lrecv.at[d], tm=lax.rem(t + d, nt))
        )
    for d in range(1, nt):
        pl.when(t + d < nt)(shares[d].start)

    local[5].wait()
    local[6].wait()
    local[7].wait()
    queries = jnp.dot(latent, qwv[...], preferred_element_type=f32).astype(bf16).astype(f32)
    width = latent.shape[1]
    group = headsv.shape[0]
    for d in range(nt):
        if d:
            pl.when(t >= d)(shares[d].wait_recv)
        keys = jnp.dot(gl[d], kwv[...], preferred_element_type=f32).astype(bf16).astype(f32)
        product = queries * keys
        high = product.astype(bf16)
        low = (product - high.astype(f32)).astype(bf16)
        for c in range(width // group):
            part = slice(c * group, (c + 1) * group)
            score = jnp.dot(high[:, part], headsv[...], preferred_element_type=f32)
            score += jnp.dot(low[:, part], headsv[...], preferred_element_type=f32)
            score = score * HEAD_DIM ** (-0.5)
            sc[d, :, part] = score if d == 0 else jnp.where(t >= d, score, -1e30)
    top = sc[0]
    for d in range(1, nt):
        top = jnp.maximum(top, sc[d])
    denominator = jnp.zeros_like(top)
    for d in range(nt):
        weight = jnp.exp(sc[d] - top)
        sc[d] = weight
        denominator += weight
    mixed = jnp.zeros_like(top)
    for d in range(nt):
        mixed += (sc[d] / denominator).astype(bf16).astype(f32) * gl[d].astype(f32)
    result = latent.astype(f32) + mixed.astype(bf16).astype(f32)
    out[...] = result.astype(bf16).reshape(out.shape)

    for i in range(2):
        pl.when(sends[i])(halo[i].wait_send)
        pl.when(has_past & sends[i])(relay[i].wait_send)
    for copy in past:
        pl.when(has_next)(copy.wait_send)
    for copy in list(weights.values()) + list(onward.values()):
        copy.wait_send()
    for d in range(1, nt):
        pl.when(t + d < nt)(shares[d].wait_send)


def body(nh, nt, video, norm_gain, sw, tw, hw, qw, kw):
    frames, rows, cols, chan = video.shape
    outward, width = sw.shape[3], hw.shape[1]
    bf16, f32 = jnp.bfloat16, jnp.float32
    group = min(256, width)
    ids = np.arange(group) // HEAD_DIM
    heads = jnp.asarray(ids[:, None] == ids[None, :], bf16)
    haar = jnp.asarray(haar_matrix(cols), bf16)
    total, places = frames + 2, rows // 2 * (cols // 2)
    dma = pltpu.SemaphoreType.DMA
    anywhere, vmem = pl.BlockSpec(memory_space=pl.ANY), pl.BlockSpec(memory_space=pltpu.VMEM)
    return pl.pallas_call(
        functools.partial(kernel, nh, nt),
        out_shape=jax.ShapeDtypeStruct((frames // 2, rows // 2, cols // 2, width), bf16),
        in_specs=[anywhere, vmem] + [anywhere] * 7,
        out_specs=vmem,
        scratch_shapes=[
            pltpu.VMEM((total, rows + 2, cols, chan), bf16),
            pltpu.VMEM((3, 3, chan, outward), bf16),
            pltpu.VMEM(tw.shape, bf16),
            pltpu.VMEM(hw.shape, bf16),
            pltpu.VMEM(qw.shape, bf16),
            pltpu.VMEM(kw.shape, bf16),
            pltpu.VMEM(haar.shape, bf16),
            pltpu.VMEM(heads.shape, bf16),
            pltpu.VMEM((total, rows + 2, cols, 3 * chan), bf16),
            pltpu.VMEM((total, rows * cols, outward), f32),
            pltpu.VMEM((total, rows * cols, outward), bf16),
            pltpu.VMEM((frames, rows * cols, chan), bf16),
            pltpu.VMEM((places, 8 * chan), bf16),
            pltpu.VMEM((nt, places, width), bf16),
            pltpu.VMEM((nt, places, width), f32),
            dma((8,)),
            dma((nh // 2, 3)), dma((nh // 2, 3)), dma((nh // 2, 3)), dma((nh // 2, 3)),
            dma((2,)), dma((2,)), dma((2,)), dma((2,)), dma((3,)), dma((3,)),
            dma((nt,)), dma((nt,)),
        ],
        compiler_params=pltpu.CompilerParams(
            collective_id=0, has_side_effects=True, vmem_limit_bytes=40 * 1024 * 1024
        ),
        cost_estimate=pl.CostEstimate(
            flops=2 * 10**9, bytes_accessed=5 * 10**6, transcendentals=10**6
        ),
    )(video, norm_gain.reshape(1, chan), sw, tw, hw, qw, kw, haar, heads)


def solution(mesh):
    in_specs = (
        P(("groups", "tm"), "height", None, None),
        P(),
        P(None, None, "height", None),
        P(),
        P(),
        P(),
        P(),
    )
    out_specs = P(("groups", "tm"), "height", None, None)
    run = functools.partial(body, mesh.shape["height"], mesh.shape["tm"])
    return jax.shard_map(run, mesh=mesh, in_specs=in_specs, out_specs=out_specs, check_vma=False)
```

```python
import functools

import jax
import jax.numpy as jnp
import numpy as np
from jax import lax
from jax.experimental import pallas as pl
from jax.experimental.pallas import tpu as pltpu
from jax.sharding import PartitionSpec as P

HEAD_DIM = 64
epsilon = 1e-06
inv_root = 0.7071067811865476
MESH = pl.DeviceIdType.MESH


def haar_matrix(cols):
    half = cols // 2
    band = np.arange(4 * cols)[:, None] // half
    place = np.arange(4 * cols)[:, None] % half
    item = np.arange(4 * cols)[None, :]
    frame, row, col = item // (2 * cols), (item // cols) % 2, item % cols
    odd = (band // 4) * frame + ((band // 2) % 2) * row + (band % 2) * (col % 2)
    return np.where(col // 2 == place, np.where(odd % 2 == 1, -1.0, 1.0), 0.0)


def kernel(
    nh, nt, video, gain, sw, tw, hw, qw, kw, haar, heads, out,
    vid, wfull, twv, hwv, qwv, kwv, haarv, headsv, patches, acc, sp, mg, bands, gl, sc,
    local_sem, wsend, wrecv, fsend, frecv, hsend, hrecv, gsend, grecv, vsend, vrecv, lsend, lrecv,
):
    h, t = lax.axis_index("height"), lax.axis_index("tm")
    frames, rows, cols, chan = video.shape
    cin = sw.shape[2]
    chips = nh // 2
    chip, core = lax.div(h, 2), lax.rem(h, 2)
    sibling = chip * 2 + 1 - core
    f32, bf16 = jnp.float32, jnp.bfloat16

    def remote(src, dst, send, recv, **where):
        return pltpu.make_async_remote_copy(
            src_ref=src, dst_ref=dst, send_sem=send, recv_sem=recv, device_id=where, device_id_type=MESH
        )

    own_in = pl.ds(pl.multiple_of(h * cin, cin), cin)
    local = [
        pltpu.make_async_copy(video, vid.at[pl.ds(2, frames), pl.ds(1, rows)], local_sem.at[0]),
        pltpu.make_async_copy(sw, wfull.at[:, :, own_in, :], local_sem.at[1]),
        pltpu.make_async_copy(tw, twv, local_sem.at[2]),
        pltpu.make_async_copy(haar, haarv, local_sem.at[3]),
        pltpu.make_async_copy(hw, hwv, local_sem.at[4]),
        pltpu.make_async_copy(qw, qwv, local_sem.at[5]),
        pltpu.make_async_copy(kw, kwv, local_sem.at[6]),
        pltpu.make_async_copy(heads, headsv, local_sem.at[7]),
    ]
    for copy in local:
        copy.start()

    barrier = pltpu.get_barrier_semaphore()
    for d in range(1, nh):
        pl.semaphore_signal(barrier, inc=1, device_id={"height": lax.rem(h + d, nh)}, device_id_type=MESH)
    for d in range(1, nt):
        pl.semaphore_signal(barrier, inc=1, device_id={"tm": lax.rem(t + d, nt)}, device_id_type=MESH)

    total = frames + 2
    for edge, slot in ((0, 0), (nh - 1, rows + 1)):
        @pl.when(h == edge)
        def _():
            vid[:, slot] = jnp.zeros((total, cols, chan), bf16)

    @pl.when(t == 0)
    def _():
        for f in range(2):
            vid[f] = jnp.zeros((rows + 2, cols, chan), bf16)

    for d in range(1, nt):
        @pl.when(t < d)
        def _():
            gl[d] = jnp.zeros(gl.shape[1:], bf16)

    pl.semaphore_wait(barrier, nh - 1 + nt - 1)

    later = {"tm": lax.rem(t + 1, nt)}
    above, below = {"height": lax.rem(h + nh - 1, nh)}, {"height": lax.rem(h + 1, nh)}
    tail = video.at[pl.ds(frames - 2, 2)]
    mine = pl.ds(2, frames)
    halo = [
        remote(video.at[:, 0], vid.at[mine, rows + 1], hsend.at[0], hrecv.at[0], **above),
        remote(video.at[:, rows - 1], vid.at[mine, 0], hsend.at[1], hrecv.at[1], **below),
    ]
    past = [
        remote(tail.at[:, 0], vid.at[pl.ds(0, 2), 1], vsend.at[0], vrecv.at[0], **later),
        remote(tail.at[:, rows - 1], vid.at[pl.ds(0, 2), rows], vsend.at[1], vrecv.at[1], **later),
        remote(
            tail.at[:, pl.ds(1, rows - 2)], vid.at[pl.ds(0, 2), pl.ds(2, rows - 2)],
            vsend.at[2], vrecv.at[2], **later,
        ),
    ]
    relay = [
        remote(vid.at[pl.ds(0, 2), 1], vid.at[pl.ds(0, 2), rows + 1], gsend.at[0], grecv.at[0], **above),
        remote(vid.at[pl.ds(0, 2), rows], vid.at[pl.ds(0, 2), 0], gsend.at[1], grecv.at[1], **below),
    ]
    up, down, has_past, has_next = h > 0, h < nh - 1, t > 0, t < nt - 1
    sends = (up, down)
    receives = (down, up)

    weights, onward = {}, {}
    for a in range(3):
        piece = wfull.at[a, :, own_in, :]
        weights[0, a] = remote(
            sw.at[a], piece, wsend.at[0, a], wrecv.at[0, a], height=sibling
        )
        for d in range(1, chips):
            weights[d, a] = remote(
                sw.at[a], piece, wsend.at[d, a], wrecv.at[d, a],
                height=lax.rem(chip + d, chips) * 2 + core,
            )
            origin = lax.rem(chip + chips - d, chips) * 2 + core
            held = wfull.at[a, :, pl.ds(pl.multiple_of(origin * cin, cin), cin), :]
            onward[d, a] = remote(held, held, fsend.at[d, a], frecv.at[d, a], height=sibling)

    for cond, copy in zip(sends, halo):
        pl.when(cond)(copy.start)
    for copy in past:
        pl.when(has_next)(copy.start)
    for a in range(3):
        for d in range(1, chips):
            weights[d, a].start()
        weights[0, a].start()

    column = lax.broadcasted_iota(jnp.int32, (cols, chan), 0)
    scale = gain[...]

    def activate(f, r):
        values = vid[f, r].astype(f32)
        square = jnp.mean(values * values, axis=-1, keepdims=True)
        normed = values * lax.rsqrt(square + epsilon) * scale
        acted = normed * jax.nn.sigmoid(normed)
        before = jnp.where(column == 0, 0.0, pltpu.roll(acted, 1, 0))
        after = jnp.where(column == cols - 1, 0.0, pltpu.roll(acted, cols - 1, 0))
        patches[f, r, :, pl.ds(0, chan)] = before.astype(bf16)
        patches[f, r, :, pl.ds(chan, chan)] = acted.astype(bf16)
        patches[f, r, :, pl.ds(2 * chan, chan)] = after.astype(bf16)

    def activate_rows(first, count, row, height):
        def step(i, carry):
            activate(first + lax.div(i, height), row + lax.rem(i, height))
            return carry
        lax.fori_loop(0, count * height, step, 0)

    def receive(copies):
        for copy in copies:
            copy.wait_recv()

    local[0].wait()
    activate_rows(2, frames, 1, rows)
    for i in range(2):
        pl.when(has_past)(past[i].wait_recv)
        pl.when(has_past & sends[i])(relay[i].start)
    for i, row in ((0, rows + 1), (1, 0)):
        pl.when(receives[i])(halo[i].wait_recv)
        activate_rows(2, frames, row, 1)
    for d in range(1, chips):
        weights[d, 0].wait_recv()
        onward[d, 0].start()
    pl.when(has_past)(past[2].wait_recv)
    activate_rows(0, 2, 1, rows)
    for d in range(1, chips):
        weights[d, 1].wait_recv()
        onward[d, 1].start()
    for i, row in ((0, rows + 1), (1, 0)):
        pl.when(has_past & receives[i])(relay[i].wait_recv)
        activate_rows(0, 2, row, 1)
    local[1].wait()
    for a in range(3):
        if a == 1:
            for d in range(1, chips):
                weights[d, 2].wait_recv()
                onward[d, 2].start()
        weights[0, a].wait_recv()
        receive([onward[d, a] for d in range(1, chips)])
        taps = wfull[a].reshape(3 * chan, wfull.shape[3])
        for f in range(total):
            part = jnp.dot(
                patches[f, a : a + rows].reshape(rows * cols, 3 * chan), taps,
                preferred_element_type=f32,
            )
            if a == 0:
                acc[f] = part
            elif a == 1:
                acc[f] += part
            else:
                sp[f] = (acc[f] + part).astype(bf16)

    local[2].wait()
    for f in range(frames):
        temporal = jnp.dot(sp[f], twv[0], preferred_element_type=f32)
        for k in (1, 2):
            temporal += jnp.dot(sp[f + k], twv[k], preferred_element_type=f32)
        own = vid[f + 2, 1 : rows + 1].reshape(rows * cols, chan).astype(f32)
        mg[f] = (own + temporal).astype(bf16)

    local[3].wait()
    half = cols // 2
    for j in range(rows // 2):
        pair = pl.ds(2 * j * cols, 2 * cols)
        block = jnp.concatenate([mg[0, pair], mg[1, pair]], axis=0)
        split = jnp.dot(haarv[...], block, preferred_element_type=f32) * (inv_root * inv_root * inv_root)
        for band in range(8):
            bands[pl.ds(j * half, half), pl.ds(band * chan, chan)] = split[
                band * half : (band + 1) * half
            ].astype(bf16)
    local[4].wait()
    latent = jnp.dot(bands[...], hwv[...], preferred_element_type=f32).astype(bf16)
    gl[0] = latent

    shares = [None]
    for d in range(1, nt):
        shares.append(
            remote(gl.at[0], gl.at[d], lsend.at[d], lrecv.at[d], tm=lax.rem(t + d, nt))
        )
    for d in range(1, nt):
        pl.when(t + d < nt)(shares[d].start)

    local[5].wait()
    local[6].wait()
    local[7].wait()
    queries = jnp.dot(latent, qwv[...], preferred_element_type=f32).astype(bf16).astype(f32)
    width = latent.shape[1]
    group = headsv.shape[0]
    for d in range(nt):
        if d:
            pl.when(t >= d)(shares[d].wait_recv)
        keys = jnp.dot(gl[d], kwv[...], preferred_element_type=f32).astype(bf16).astype(f32)
        product = queries * keys
        high = product.astype(bf16)
        low = (product - high.astype(f32)).astype(bf16)
        for c in range(width // group):
            part = slice(c * group, (c + 1) * group)
            score = jnp.dot(high[:, part], headsv[...], preferred_element_type=f32)
            score += jnp.dot(low[:, part], headsv[...], preferred_element_type=f32)
            score = score * HEAD_DIM ** (-0.5)
            sc[d, :, part] = score if d == 0 else jnp.where(t >= d, score, -1e30)
    top = sc[0]
    for d in range(1, nt):
        top = jnp.maximum(top, sc[d])
    denominator = jnp.zeros_like(top)
    for d in range(nt):
        weight = jnp.exp(sc[d] - top)
        sc[d] = weight
        denominator += weight
    mixed = jnp.zeros_like(top)
    for d in range(nt):
        mixed += (sc[d] / denominator).astype(bf16).astype(f32) * gl[d].astype(f32)
    result = latent.astype(f32) + mixed.astype(bf16).astype(f32)
    out[...] = result.astype(bf16).reshape(out.shape)

    for i in range(2):
        pl.when(sends[i])(halo[i].wait_send)
        pl.when(has_past & sends[i])(relay[i].wait_send)
    for copy in past:
        pl.when(has_next)(copy.wait_send)
    for copy in list(weights.values()) + list(onward.values()):
        copy.wait_send()
    for d in range(1, nt):
        pl.when(t + d < nt)(shares[d].wait_send)


def body(nh, nt, video, norm_gain, sw, tw, hw, qw, kw):
    frames, rows, cols, chan = video.shape
    outward, width = sw.shape[3], hw.shape[1]
    bf16, f32 = jnp.bfloat16, jnp.float32
    group = min(256, width)
    ids = np.arange(group) // HEAD_DIM
    heads = jnp.asarray(ids[:, None] == ids[None, :], bf16)
    haar = jnp.asarray(haar_matrix(cols), bf16)
    total, places = frames + 2, rows // 2 * (cols // 2)
    dma = pltpu.SemaphoreType.DMA
    anywhere, vmem = pl.BlockSpec(memory_space=pltpu.HBM), pl.BlockSpec(memory_space=pltpu.VMEM)
    return pl.pallas_call(
        functools.partial(kernel, nh, nt),
        out_shape=jax.ShapeDtypeStruct((frames // 2, rows // 2, cols // 2, width), bf16),
        in_specs=[anywhere, vmem] + [anywhere] * 7,
        out_specs=vmem,
        scratch_shapes=[
            pltpu.VMEM((total, rows + 2, cols, chan), bf16),
            pltpu.VMEM((3, 3, chan, outward), bf16),
            pltpu.VMEM(tw.shape, bf16),
            pltpu.VMEM(hw.shape, bf16),
            pltpu.VMEM(qw.shape, bf16),
            pltpu.VMEM(kw.shape, bf16),
            pltpu.VMEM(haar.shape, bf16),
            pltpu.VMEM(heads.shape, bf16),
            pltpu.VMEM((total, rows + 2, cols, 3 * chan), bf16),
            pltpu.VMEM((total, rows * cols, outward), f32),
            pltpu.VMEM((total, rows * cols, outward), bf16),
            pltpu.VMEM((frames, rows * cols, chan), bf16),
            pltpu.VMEM((places, 8 * chan), bf16),
            pltpu.VMEM((nt, places, width), bf16),
            pltpu.VMEM((nt, places, width), f32),
            dma((8,)),
            dma((nh // 2, 3)), dma((nh // 2, 3)), dma((nh // 2, 3)), dma((nh // 2, 3)),
            dma((2,)), dma((2,)), dma((2,)), dma((2,)), dma((3,)), dma((3,)),
            dma((nt,)), dma((nt,)),
        ],
        compiler_params=pltpu.CompilerParams(
            collective_id=0, has_side_effects=True, vmem_limit_bytes=60 * 1024 * 1024
        ),
        cost_estimate=pl.CostEstimate(
            flops=2 * 10**9, bytes_accessed=5 * 10**6, transcendentals=10**6
        ),
    )(video, norm_gain.reshape(1, chan), sw, tw, hw, qw, kw, haar, heads)


def solution(mesh):
    in_specs = (
        P(("groups", "tm"), "height", None, None),
        P(),
        P(None, None, "height", None),
        P(),
        P(),
        P(),
        P(),
    )
    out_specs = P(("groups", "tm"), "height", None, None)
    run = functools.partial(body, mesh.shape["height"], mesh.shape["tm"])
    return jax.shard_map(run, mesh=mesh, in_specs=in_specs, out_specs=out_specs, check_vma=False)
```

```python
import functools

import jax
import jax.numpy as jnp
import numpy as np
from jax import lax
from jax.experimental import pallas as pl
from jax.experimental.pallas import tpu as pltpu
from jax.sharding import PartitionSpec as P

HEAD_DIM = 64
epsilon = 1e-06
inv_root = 0.7071067811865476
MESH = pl.DeviceIdType.MESH


def haar_matrix(cols):
    half = cols // 2
    band = np.arange(4 * cols)[:, None] // half
    place = np.arange(4 * cols)[:, None] % half
    item = np.arange(4 * cols)[None, :]
    frame, row, col = item // (2 * cols), (item // cols) % 2, item % cols
    odd = (band // 4) * frame + ((band // 2) % 2) * row + (band % 2) * (col % 2)
    return np.where(col // 2 == place, np.where(odd % 2 == 1, -1.0, 1.0), 0.0)


def kernel(
    nh, nt, video, gain, sw, tw, hw, qw, kw, haar, heads, out,
    vid, wfull, twv, hwv, qwv, kwv, haarv, headsv, patches, acc, sp, mg, bands, gl, sc,
    local_sem, wsend, wrecv, fsend, frecv, hsend, hrecv, gsend, grecv, vsend, vrecv, lsend, lrecv,
):
    h, t = lax.axis_index("height"), lax.axis_index("tm")
    frames, rows, cols, chan = video.shape
    cin = sw.shape[2]
    chips = nh // 2
    chip, core = lax.div(h, 2), lax.rem(h, 2)
    sibling = chip * 2 + 1 - core
    f32, bf16 = jnp.float32, jnp.bfloat16

    def remote(src, dst, send, recv, **where):
        return pltpu.make_async_remote_copy(
            src_ref=src, dst_ref=dst, send_sem=send, recv_sem=recv, device_id=where, device_id_type=MESH
        )

    own_in = pl.ds(pl.multiple_of(h * cin, cin), cin)
    local = [
        pltpu.make_async_copy(video, vid.at[pl.ds(2, frames), pl.ds(1, rows)], local_sem.at[0]),
        pltpu.make_async_copy(sw, wfull.at[:, :, own_in, :], local_sem.at[1]),
        pltpu.make_async_copy(tw, twv, local_sem.at[2]),
        pltpu.make_async_copy(haar, haarv, local_sem.at[3]),
        pltpu.make_async_copy(hw, hwv, local_sem.at[4]),
        pltpu.make_async_copy(qw, qwv, local_sem.at[5]),
        pltpu.make_async_copy(kw, kwv, local_sem.at[6]),
        pltpu.make_async_copy(heads, headsv, local_sem.at[7]),
    ]
    for copy in local:
        copy.start()

    barrier = pltpu.get_barrier_semaphore()
    for d in range(1, nh):
        pl.semaphore_signal(barrier, inc=1, device_id={"height": lax.rem(h + d, nh)}, device_id_type=MESH)
    for d in range(1, nt):
        pl.semaphore_signal(barrier, inc=1, device_id={"tm": lax.rem(t + d, nt)}, device_id_type=MESH)

    total = frames + 2
    for edge, slot in ((0, 0), (nh - 1, rows + 1)):
        @pl.when(h == edge)
        def _():
            vid[:, slot] = jnp.zeros((total, cols, chan), bf16)

    @pl.when(t == 0)
    def _():
        for f in range(2):
            vid[f] = jnp.zeros((rows + 2, cols, chan), bf16)

    for d in range(1, nt):
        @pl.when(t < d)
        def _():
            gl[d] = jnp.zeros(gl.shape[1:], bf16)

    pl.semaphore_wait(barrier, nh - 1 + nt - 1)

    later = {"tm": lax.rem(t + 1, nt)}
    above, below = {"height": lax.rem(h + nh - 1, nh)}, {"height": lax.rem(h + 1, nh)}
    tail = video.at[pl.ds(frames - 2, 2)]
    mine = pl.ds(2, frames)
    halo = [
        remote(video.at[:, 0], vid.at[mine, rows + 1], hsend.at[0], hrecv.at[0], **above),
        remote(video.at[:, rows - 1], vid.at[mine, 0], hsend.at[1], hrecv.at[1], **below),
    ]
    past = [
        remote(tail.at[:, 0], vid.at[pl.ds(0, 2), 1], vsend.at[0], vrecv.at[0], **later),
        remote(tail.at[:, rows - 1], vid.at[pl.ds(0, 2), rows], vsend.at[1], vrecv.at[1], **later),
        remote(
            tail.at[:, pl.ds(1, rows - 2)], vid.at[pl.ds(0, 2), pl.ds(2, rows - 2)],
            vsend.at[2], vrecv.at[2], **later,
        ),
    ]
    relay = [
        remote(vid.at[pl.ds(0, 2), 1], vid.at[pl.ds(0, 2), rows + 1], gsend.at[0], grecv.at[0], **above),
        remote(vid.at[pl.ds(0, 2), rows], vid.at[pl.ds(0, 2), 0], gsend.at[1], grecv.at[1], **below),
    ]
    up, down, has_past, has_next = h > 0, h < nh - 1, t > 0, t < nt - 1
    sends = (up, down)
    receives = (down, up)

    weights, onward = {}, {}
    for a in range(3):
        piece = wfull.at[a, :, own_in, :]
        weights[0, a] = remote(
            sw.at[a], piece, wsend.at[0, a], wrecv.at[0, a], height=sibling
        )
        for d in range(1, chips):
            weights[d, a] = remote(
                sw.at[a], piece, wsend.at[d, a], wrecv.at[d, a],
                height=lax.rem(chip + d, chips) * 2 + core,
            )
            origin = lax.rem(chip + chips - d, chips) * 2 + core
            held = wfull.at[a, :, pl.ds(pl.multiple_of(origin * cin, cin), cin), :]
            onward[d, a] = remote(held, held, fsend.at[d, a], frecv.at[d, a], height=sibling)

    for cond, copy in zip(sends, halo):
        pl.when(cond)(copy.start)
    for copy in past:
        pl.when(has_next)(copy.start)
    for a in range(3):
        for d in range(1, chips):
            weights[d, a].start()
        weights[0, a].start()

    column = lax.broadcasted_iota(jnp.int32, (cols, chan), 0)
    scale = gain[...]

    def activate(f, r):
        values = vid[f, r].astype(f32)
        square = jnp.mean(values * values, axis=-1, keepdims=True)
        normed = values * lax.rsqrt(square + epsilon) * scale
        acted = normed * jax.nn.sigmoid(normed)
        before = jnp.where(column == 0, 0.0, pltpu.roll(acted, 1, 0))
        after = jnp.where(column == cols - 1, 0.0, pltpu.roll(acted, cols - 1, 0))
        patches[f, r, :, pl.ds(0, chan)] = before.astype(bf16)
        patches[f, r, :, pl.ds(chan, chan)] = acted.astype(bf16)
        patches[f, r, :, pl.ds(2 * chan, chan)] = after.astype(bf16)

    def activate_rows(first, count, row, height):
        def step(i, carry):
            activate(first + lax.div(i, height), row + lax.rem(i, height))
            return carry
        lax.fori_loop(0, count * height, step, 0)

    def receive(copies):
        for copy in copies:
            copy.wait_recv()

    local[0].wait()
    activate_rows(2, frames, 1, rows)
    for i in range(2):
        pl.when(has_past)(past[i].wait_recv)
        pl.when(has_past & sends[i])(relay[i].start)
    for i, row in ((0, rows + 1), (1, 0)):
        pl.when(receives[i])(halo[i].wait_recv)
        activate_rows(2, frames, row, 1)
    for d in range(1, chips):
        weights[d, 0].wait_recv()
        onward[d, 0].start()
    pl.when(has_past)(past[2].wait_recv)
    activate_rows(0, 2, 1, rows)
    for d in range(1, chips):
        weights[d, 1].wait_recv()
        onward[d, 1].start()
    for i, row in ((0, rows + 1), (1, 0)):
        pl.when(has_past & receives[i])(relay[i].wait_recv)
        activate_rows(0, 2, row, 1)
    local[1].wait()
    for a in range(3):
        if a == 1:
            for d in range(1, chips):
                weights[d, 2].wait_recv()
                onward[d, 2].start()
        weights[0, a].wait_recv()
        receive([onward[d, a] for d in range(1, chips)])
        taps = wfull[a].reshape(3 * chan, wfull.shape[3])
        for f in range(total):
            part = jnp.dot(
                patches[f, a : a + rows].reshape(rows * cols, 3 * chan), taps,
                preferred_element_type=f32,
            )
            if a == 0:
                acc[f] = part
            elif a == 1:
                acc[f] += part
            else:
                sp[f] = (acc[f] + part).astype(bf16)

    local[2].wait()
    for f in range(frames):
        temporal = jnp.dot(sp[f], twv[0], preferred_element_type=f32)
        for k in (1, 2):
            temporal += jnp.dot(sp[f + k], twv[k], preferred_element_type=f32)
        own = vid[f + 2, 1 : rows + 1].reshape(rows * cols, chan).astype(f32)
        mg[f] = (own + temporal).astype(bf16)

    local[3].wait()
    half = cols // 2
    for j in range(rows // 2):
        pair = pl.ds(2 * j * cols, 2 * cols)
        block = jnp.concatenate([mg[0, pair], mg[1, pair]], axis=0)
        split = jnp.dot(haarv[...], block, preferred_element_type=f32) * (inv_root * inv_root * inv_root)
        for band in range(8):
            bands[pl.ds(j * half, half), pl.ds(band * chan, chan)] = split[
                band * half : (band + 1) * half
            ].astype(bf16)
    local[4].wait()
    latent = jnp.dot(bands[...], hwv[...], preferred_element_type=f32).astype(bf16)
    gl[0] = latent

    shares = [None]
    for d in range(1, nt):
        shares.append(
            remote(gl.at[0], gl.at[d], lsend.at[d], lrecv.at[d], tm=lax.rem(t + d, nt))
        )
    for d in range(nt - 1, 0, -1):
        pl.when(t + d < nt)(shares[d].start)

    local[5].wait()
    local[6].wait()
    local[7].wait()
    queries = jnp.dot(latent, qwv[...], preferred_element_type=f32).astype(bf16).astype(f32)
    width = latent.shape[1]
    group = headsv.shape[0]
    for d in range(nt):
        if d:
            pl.when(t >= d)(shares[d].wait_recv)
        keys = jnp.dot(gl[d], kwv[...], preferred_element_type=f32).astype(bf16).astype(f32)
        product = queries * keys
        high = product.astype(bf16)
        low = (product - high.astype(f32)).astype(bf16)
        for c in range(width // group):
            part = slice(c * group, (c + 1) * group)
            score = jnp.dot(high[:, part], headsv[...], preferred_element_type=f32)
            score += jnp.dot(low[:, part], headsv[...], preferred_element_type=f32)
            score = score * HEAD_DIM ** (-0.5)
            sc[d, :, part] = score if d == 0 else jnp.where(t >= d, score, -1e30)
    top = sc[0]
    for d in range(1, nt):
        top = jnp.maximum(top, sc[d])
    denominator = jnp.zeros_like(top)
    for d in range(nt):
        weight = jnp.exp(sc[d] - top)
        sc[d] = weight
        denominator += weight
    mixed = jnp.zeros_like(top)
    for d in range(nt):
        mixed += (sc[d] / denominator).astype(bf16).astype(f32) * gl[d].astype(f32)
    result = latent.astype(f32) + mixed.astype(bf16).astype(f32)
    out[...] = result.astype(bf16).reshape(out.shape)

    for i in range(2):
        pl.when(sends[i])(halo[i].wait_send)
        pl.when(has_past & sends[i])(relay[i].wait_send)
    for copy in past:
        pl.when(has_next)(copy.wait_send)
    for copy in list(weights.values()) + list(onward.values()):
        copy.wait_send()
    for d in range(1, nt):
        pl.when(t + d < nt)(shares[d].wait_send)


def body(nh, nt, video, norm_gain, sw, tw, hw, qw, kw):
    frames, rows, cols, chan = video.shape
    outward, width = sw.shape[3], hw.shape[1]
    bf16, f32 = jnp.bfloat16, jnp.float32
    group = min(256, width)
    ids = np.arange(group) // HEAD_DIM
    heads = jnp.asarray(ids[:, None] == ids[None, :], bf16)
    haar = jnp.asarray(haar_matrix(cols), bf16)
    total, places = frames + 2, rows // 2 * (cols // 2)
    dma = pltpu.SemaphoreType.DMA
    anywhere, vmem = pl.BlockSpec(memory_space=pltpu.HBM), pl.BlockSpec(memory_space=pltpu.VMEM)
    return pl.pallas_call(
        functools.partial(kernel, nh, nt),
        out_shape=jax.ShapeDtypeStruct((frames // 2, rows // 2, cols // 2, width), bf16),
        in_specs=[anywhere, vmem] + [anywhere] * 7,
        out_specs=vmem,
        scratch_shapes=[
            pltpu.VMEM((total, rows + 2, cols, chan), bf16),
            pltpu.VMEM((3, 3, chan, outward), bf16),
            pltpu.VMEM(tw.shape, bf16),
            pltpu.VMEM(hw.shape, bf16),
            pltpu.VMEM(qw.shape, bf16),
            pltpu.VMEM(kw.shape, bf16),
            pltpu.VMEM(haar.shape, bf16),
            pltpu.VMEM(heads.shape, bf16),
            pltpu.VMEM((total, rows + 2, cols, 3 * chan), bf16),
            pltpu.VMEM((total, rows * cols, outward), f32),
            pltpu.VMEM((total, rows * cols, outward), bf16),
            pltpu.VMEM((frames, rows * cols, chan), bf16),
            pltpu.VMEM((places, 8 * chan), bf16),
            pltpu.VMEM((nt, places, width), bf16),
            pltpu.VMEM((nt, places, width), f32),
            dma((8,)),
            dma((nh // 2, 3)), dma((nh // 2, 3)), dma((nh // 2, 3)), dma((nh // 2, 3)),
            dma((2,)), dma((2,)), dma((2,)), dma((2,)), dma((3,)), dma((3,)),
            dma((nt,)), dma((nt,)),
        ],
        compiler_params=pltpu.CompilerParams(
            collective_id=0, has_side_effects=True, vmem_limit_bytes=40 * 1024 * 1024
        ),
        cost_estimate=pl.CostEstimate(
            flops=2 * 10**9, bytes_accessed=5 * 10**6, transcendentals=10**6
        ),
    )(video, norm_gain.reshape(1, chan), sw, tw, hw, qw, kw, haar, heads)


def solution(mesh):
    in_specs = (
        P(("groups", "tm"), "height", None, None),
        P(),
        P(None, None, "height", None),
        P(),
        P(),
        P(),
        P(),
    )
    out_specs = P(("groups", "tm"), "height", None, None)
    run = functools.partial(body, mesh.shape["height"], mesh.shape["tm"])
    return jax.shard_map(run, mesh=mesh, in_specs=in_specs, out_specs=out_specs, check_vma=False)
```

```python
import functools

import jax
import jax.numpy as jnp
import numpy as np
from jax import lax
from jax.experimental import pallas as pl
from jax.experimental.pallas import tpu as pltpu
from jax.sharding import PartitionSpec as P

HEAD_DIM = 64
epsilon = 1e-06
inv_root = 0.7071067811865476
MESH = pl.DeviceIdType.MESH


def haar_matrix(cols):
    half = cols // 2
    band = np.arange(4 * cols)[:, None] // half
    place = np.arange(4 * cols)[:, None] % half
    item = np.arange(4 * cols)[None, :]
    frame, row, col = item // (2 * cols), (item // cols) % 2, item % cols
    odd = (band // 4) * frame + ((band // 2) % 2) * row + (band % 2) * (col % 2)
    return np.where(col // 2 == place, np.where(odd % 2 == 1, -1.0, 1.0), 0.0)


def kernel(
    nh, nt, ng, video, gain, sw, tw, hw, qw, kw, haar, heads, out,
    vid, wfull, twv, hwv, qwv, kwv, haarv, headsv, patches, acc, sp, mg, bands, gl, sc,
    local_sem, wsend, wrecv, fsend, frecv, hsend, hrecv, gsend, grecv, vsend, vrecv, lsend, lrecv,
    asend, arecv, ssend, srecv,
):
    h, t, g = lax.axis_index("height"), lax.axis_index("tm"), lax.axis_index("groups")
    frames, rows, cols, chan = video.shape
    cin = sw.shape[2]
    chips = nh // 2
    chip, core = lax.div(h, 2), lax.rem(h, 2)
    sibling = chip * 2 + 1 - core
    f32, bf16 = jnp.float32, jnp.bfloat16

    def remote(src, dst, send, recv, **where):
        return pltpu.make_async_remote_copy(
            src_ref=src, dst_ref=dst, send_sem=send, recv_sem=recv, device_id=where, device_id_type=MESH
        )

    own_in = pl.ds(pl.multiple_of(h * cin, cin), cin)
    local = [
        pltpu.make_async_copy(video, vid.at[pl.ds(2, frames), pl.ds(1, rows)], local_sem.at[0]),
        pltpu.make_async_copy(sw, wfull.at[:, :, own_in, :], local_sem.at[1]),
        pltpu.make_async_copy(tw, twv, local_sem.at[2]),
        pltpu.make_async_copy(haar, haarv, local_sem.at[3]),
        pltpu.make_async_copy(hw, hwv, local_sem.at[4]),
        pltpu.make_async_copy(qw, qwv, local_sem.at[5]),
        pltpu.make_async_copy(kw, kwv, local_sem.at[6]),
        pltpu.make_async_copy(heads, headsv, local_sem.at[7]),
    ]
    for copy in local:
        copy.start()

    barrier = pltpu.get_barrier_semaphore()
    for d in range(1, nh):
        pl.semaphore_signal(barrier, inc=1, device_id={"height": lax.rem(h + d, nh)}, device_id_type=MESH)
    for d in range(1, nt):
        pl.semaphore_signal(barrier, inc=1, device_id={"tm": lax.rem(t + d, nt)}, device_id_type=MESH)

    for d in range(1, ng):
        pl.semaphore_signal(barrier, inc=1, device_id={"groups": lax.rem(g + d, ng)}, device_id_type=MESH)

    total = frames + 2
    for edge, slot in ((0, 0), (nh - 1, rows + 1)):
        @pl.when(h == edge)
        def _():
            vid[:, slot] = jnp.zeros((total, cols, chan), bf16)

    @pl.when(t == 0)
    def _():
        for f in range(2):
            vid[f] = jnp.zeros((rows + 2, cols, chan), bf16)

    for d in range(1, nt):
        @pl.when(t < d)
        def _():
            gl[d] = jnp.zeros(gl.shape[1:], bf16)

    pl.semaphore_wait(barrier, nh - 1 + nt - 1 + ng - 1)

    later = {"tm": lax.rem(t + 1, nt)}
    above, below = {"height": lax.rem(h + nh - 1, nh)}, {"height": lax.rem(h + 1, nh)}
    tail = video.at[pl.ds(frames - 2, 2)]
    mine = pl.ds(2, frames)
    halo = [
        remote(video.at[:, 0], vid.at[mine, rows + 1], hsend.at[0], hrecv.at[0], **above),
        remote(video.at[:, rows - 1], vid.at[mine, 0], hsend.at[1], hrecv.at[1], **below),
    ]
    past = [
        remote(tail.at[:, 0], vid.at[pl.ds(0, 2), 1], vsend.at[0], vrecv.at[0], **later),
        remote(tail.at[:, rows - 1], vid.at[pl.ds(0, 2), rows], vsend.at[1], vrecv.at[1], **later),
        remote(
            tail.at[:, pl.ds(1, rows - 2)], vid.at[pl.ds(0, 2), pl.ds(2, rows - 2)],
            vsend.at[2], vrecv.at[2], **later,
        ),
    ]
    relay = [
        remote(vid.at[pl.ds(0, 2), 1], vid.at[pl.ds(0, 2), rows + 1], gsend.at[0], grecv.at[0], **above),
        remote(vid.at[pl.ds(0, 2), rows], vid.at[pl.ds(0, 2), 0], gsend.at[1], grecv.at[1], **below),
    ]
    up, down, has_past, has_next = h > 0, h < nh - 1, t > 0, t < nt - 1
    sends = (up, down)
    receives = (down, up)

    part = cin // ng
    weights, onward, across, second = {}, {}, {}, {}
    for a in range(3):
        weights[0, a] = remote(
            sw.at[a], wfull.at[a, :, own_in, :], wsend.at[0, a], wrecv.at[0, a], height=sibling
        )
        for d in range(1, chips):
            mine_in = pl.ds(pl.multiple_of(h * cin + g * part, part), part)
            weights[d, a] = remote(
                sw.at[a, :, pl.ds(pl.multiple_of(g * part, part), part), :], wfull.at[a, :, mine_in, :],
                wsend.at[d, a], wrecv.at[d, a], height=lax.rem(chip + d, chips) * 2 + core,
            )
            origin = lax.rem(chip + chips - d, chips) * 2 + core
            for e in range(ng):
                source = lax.rem(g + ng - e, ng)
                start = pl.multiple_of(origin * cin + source * part, part)
                held = wfull.at[a, :, pl.ds(start, part), :]
                if e == 0:
                    first = held
                    onward[d, a] = remote(held, held, fsend.at[d, a], frecv.at[d, a], height=sibling)
                else:
                    across[d, a, e] = remote(
                        first, first, asend.at[d, a, e], arecv.at[d, a, e], groups=lax.rem(g + e, ng)
                    )
                    second[d, a, e] = remote(
                        held, held, ssend.at[d, a, e], srecv.at[d, a, e], height=sibling
                    )

    def relay_first(a):
        for d in range(1, chips):
            weights[d, a].wait_recv()
            for e in range(1, ng):
                across[d, a, e].start()
            onward[d, a].start()

    def relay_second(a):
        for d in range(1, chips):
            for e in range(1, ng):
                across[d, a, e].wait_recv()
                second[d, a, e].start()

    for cond, copy in zip(sends, halo):
        pl.when(cond)(copy.start)
    for copy in past:
        pl.when(has_next)(copy.start)
    for a in range(3):
        for d in range(1, chips):
            weights[d, a].start()
        weights[0, a].start()

    column = lax.broadcasted_iota(jnp.int32, (cols, chan), 0)
    scale = gain[...]

    def activate(f, r):
        values = vid[f, r].astype(f32)
        square = jnp.mean(values * values, axis=-1, keepdims=True)
        normed = values * lax.rsqrt(square + epsilon) * scale
        acted = normed * jax.nn.sigmoid(normed)
        before = jnp.where(column == 0, 0.0, pltpu.roll(acted, 1, 0))
        after = jnp.where(column == cols - 1, 0.0, pltpu.roll(acted, cols - 1, 0))
        patches[f, r, :, pl.ds(0, chan)] = before.astype(bf16)
        patches[f, r, :, pl.ds(chan, chan)] = acted.astype(bf16)
        patches[f, r, :, pl.ds(2 * chan, chan)] = after.astype(bf16)

    def activate_rows(first, count, row, height):
        def step(i, carry):
            activate(first + lax.div(i, height), row + lax.rem(i, height))
            return carry
        lax.fori_loop(0, count * height, step, 0)

    def receive(copies):
        for copy in copies:
            copy.wait_recv()

    local[0].wait()
    activate_rows(2, frames, 1, rows)
    for i in range(2):
        pl.when(has_past)(past[i].wait_recv)
        pl.when(has_past & sends[i])(relay[i].start)
    for i, row in ((0, rows + 1), (1, 0)):
        pl.when(receives[i])(halo[i].wait_recv)
        activate_rows(2, frames, row, 1)
    relay_first(0)
    relay_first(1)
    relay_second(0)
    relay_first(2)
    relay_second(1)
    pl.when(has_past)(past[2].wait_recv)
    activate_rows(0, 2, 1, rows)
    relay_second(2)
    for i, row in ((0, rows + 1), (1, 0)):
        pl.when(has_past & receives[i])(relay[i].wait_recv)
        activate_rows(0, 2, row, 1)
    local[1].wait()
    for a in range(3):
        weights[0, a].wait_recv()
        receive([onward[d, a] for d in range(1, chips)])
        receive([second[d, a, e] for d in range(1, chips) for e in range(1, ng)])
        taps = wfull[a].reshape(3 * chan, wfull.shape[3])
        for f in range(total):
            part = jnp.dot(
                patches[f, a : a + rows].reshape(rows * cols, 3 * chan), taps,
                preferred_element_type=f32,
            )
            if a == 0:
                acc[f] = part
            elif a == 1:
                acc[f] += part
            else:
                sp[f] = (acc[f] + part).astype(bf16)

    local[2].wait()
    for f in range(frames):
        temporal = jnp.dot(sp[f], twv[0], preferred_element_type=f32)
        for k in (1, 2):
            temporal += jnp.dot(sp[f + k], twv[k], preferred_element_type=f32)
        own = vid[f + 2, 1 : rows + 1].reshape(rows * cols, chan).astype(f32)
        mg[f] = (own + temporal).astype(bf16)

    local[3].wait()
    half = cols // 2
    for j in range(rows // 2):
        pair = pl.ds(2 * j * cols, 2 * cols)
        block = jnp.concatenate([mg[0, pair], mg[1, pair]], axis=0)
        split = jnp.dot(haarv[...], block, preferred_element_type=f32) * (inv_root * inv_root * inv_root)
        for band in range(8):
            bands[pl.ds(j * half, half), pl.ds(band * chan, chan)] = split[
                band * half : (band + 1) * half
            ].astype(bf16)
    local[4].wait()
    latent = jnp.dot(bands[...], hwv[...], preferred_element_type=f32).astype(bf16)
    gl[0] = latent

    shares = [None]
    for d in range(1, nt):
        shares.append(
            remote(gl.at[0], gl.at[d], lsend.at[d], lrecv.at[d], tm=lax.rem(t + d, nt))
        )
    for d in range(1, nt):
        pl.when(t + d < nt)(shares[d].start)

    local[5].wait()
    local[6].wait()
    local[7].wait()
    queries = jnp.dot(latent, qwv[...], preferred_element_type=f32).astype(bf16).astype(f32)
    width = latent.shape[1]
    group = headsv.shape[0]
    for d in range(nt):
        if d:
            pl.when(t >= d)(shares[d].wait_recv)
        keys = jnp.dot(gl[d], kwv[...], preferred_element_type=f32).astype(bf16).astype(f32)
        product = queries * keys
        high = product.astype(bf16)
        low = (product - high.astype(f32)).astype(bf16)
        for c in range(width // group):
            part = slice(c * group, (c + 1) * group)
            score = jnp.dot(high[:, part], headsv[...], preferred_element_type=f32)
            score += jnp.dot(low[:, part], headsv[...], preferred_element_type=f32)
            score = score * HEAD_DIM ** (-0.5)
            sc[d, :, part] = score if d == 0 else jnp.where(t >= d, score, -1e30)
    top = sc[0]
    for d in range(1, nt):
        top = jnp.maximum(top, sc[d])
    denominator = jnp.zeros_like(top)
    for d in range(nt):
        weight = jnp.exp(sc[d] - top)
        sc[d] = weight
        denominator += weight
    mixed = jnp.zeros_like(top)
    for d in range(nt):
        mixed += (sc[d] / denominator).astype(bf16).astype(f32) * gl[d].astype(f32)
    result = latent.astype(f32) + mixed.astype(bf16).astype(f32)
    out[...] = result.astype(bf16).reshape(out.shape)

    for i in range(2):
        pl.when(sends[i])(halo[i].wait_send)
        pl.when(has_past & sends[i])(relay[i].wait_send)
    for copy in past:
        pl.when(has_next)(copy.wait_send)
    for copy in [c for group in (weights, onward, across, second) for c in group.values()]:
        copy.wait_send()
    for d in range(1, nt):
        pl.when(t + d < nt)(shares[d].wait_send)


def body(nh, nt, ng, video, norm_gain, sw, tw, hw, qw, kw):
    frames, rows, cols, chan = video.shape
    outward, width = sw.shape[3], hw.shape[1]
    bf16, f32 = jnp.bfloat16, jnp.float32
    group = min(256, width)
    ids = np.arange(group) // HEAD_DIM
    heads = jnp.asarray(ids[:, None] == ids[None, :], bf16)
    haar = jnp.asarray(haar_matrix(cols), bf16)
    total, places = frames + 2, rows // 2 * (cols // 2)
    dma = pltpu.SemaphoreType.DMA
    anywhere, vmem = pl.BlockSpec(memory_space=pltpu.HBM), pl.BlockSpec(memory_space=pltpu.VMEM)
    return pl.pallas_call(
        functools.partial(kernel, nh, nt, ng),
        out_shape=jax.ShapeDtypeStruct((frames // 2, rows // 2, cols // 2, width), bf16),
        in_specs=[anywhere, vmem] + [anywhere] * 7,
        out_specs=vmem,
        scratch_shapes=[
            pltpu.VMEM((total, rows + 2, cols, chan), bf16),
            pltpu.VMEM((3, 3, chan, outward), bf16),
            pltpu.VMEM(tw.shape, bf16),
            pltpu.VMEM(hw.shape, bf16),
            pltpu.VMEM(qw.shape, bf16),
            pltpu.VMEM(kw.shape, bf16),
            pltpu.VMEM(haar.shape, bf16),
            pltpu.VMEM(heads.shape, bf16),
            pltpu.VMEM((total, rows + 2, cols, 3 * chan), bf16),
            pltpu.VMEM((total, rows * cols, outward), f32),
            pltpu.VMEM((total, rows * cols, outward), bf16),
            pltpu.VMEM((frames, rows * cols, chan), bf16),
            pltpu.VMEM((places, 8 * chan), bf16),
            pltpu.VMEM((nt, places, width), bf16),
            pltpu.VMEM((nt, places, width), f32),
            dma((8,)),
            dma((nh // 2, 3)), dma((nh // 2, 3)), dma((nh // 2, 3)), dma((nh // 2, 3)),
            dma((2,)), dma((2,)), dma((2,)), dma((2,)), dma((3,)), dma((3,)),
            dma((nt,)), dma((nt,)),
            dma((nh // 2, 3, ng)), dma((nh // 2, 3, ng)), dma((nh // 2, 3, ng)), dma((nh // 2, 3, ng)),
        ],
        compiler_params=pltpu.CompilerParams(
            collective_id=0, has_side_effects=True, vmem_limit_bytes=60 * 1024 * 1024
        ),
        cost_estimate=pl.CostEstimate(
            flops=2 * 10**9, bytes_accessed=5 * 10**6, transcendentals=10**6
        ),
    )(video, norm_gain.reshape(1, chan), sw, tw, hw, qw, kw, haar, heads)


def solution(mesh):
    in_specs = (
        P(("groups", "tm"), "height", None, None),
        P(),
        P(None, None, "height", None),
        P(),
        P(),
        P(),
        P(),
    )
    out_specs = P(("groups", "tm"), "height", None, None)
    run = functools.partial(body, mesh.shape["height"], mesh.shape["tm"], mesh.shape["groups"])
    return jax.shard_map(run, mesh=mesh, in_specs=in_specs, out_specs=out_specs, check_vma=False)
```

```python
import functools

import jax
import jax.numpy as jnp
import numpy as np
from jax import lax
from jax.experimental import pallas as pl
from jax.experimental.pallas import tpu as pltpu
from jax.sharding import PartitionSpec as P

HEAD_DIM = 64
epsilon = 1e-06
inv_root = 0.7071067811865476
MESH = pl.DeviceIdType.MESH


def haar_matrix(cols):
    half = cols // 2
    band = np.arange(4 * cols)[:, None] // half
    place = np.arange(4 * cols)[:, None] % half
    item = np.arange(4 * cols)[None, :]
    frame, row, col = item // (2 * cols), (item // cols) % 2, item % cols
    odd = (band // 4) * frame + ((band // 2) % 2) * row + (band % 2) * (col % 2)
    return np.where(col // 2 == place, np.where(odd % 2 == 1, -1.0, 1.0), 0.0)


def kernel(
    nh, nt, video, gain, sw, tw, hw, qw, kw, haar, heads, out,
    vid, wfull, twv, hwv, qwv, kwv, haarv, headsv, patches, acc, sp, mg, bands, gl, sc,
    local_sem, wsend, wrecv, fsend, frecv, hsend, hrecv, gsend, grecv, vsend, vrecv, lsend, lrecv,
):
    h, t = lax.axis_index("height"), lax.axis_index("tm")
    frames, rows, cols, chan = video.shape
    cin = sw.shape[2]
    chips = nh // 2
    chip, core = lax.div(h, 2), lax.rem(h, 2)
    sibling = chip * 2 + 1 - core
    f32, bf16 = jnp.float32, jnp.bfloat16

    def remote(src, dst, send, recv, **where):
        return pltpu.make_async_remote_copy(
            src_ref=src, dst_ref=dst, send_sem=send, recv_sem=recv, device_id=where, device_id_type=MESH
        )

    own_in = pl.ds(pl.multiple_of(h * cin, cin), cin)
    local = [
        pltpu.make_async_copy(video, vid.at[pl.ds(2, frames), pl.ds(1, rows)], local_sem.at[0]),
        pltpu.make_async_copy(sw, wfull.at[:, :, own_in, :], local_sem.at[1]),
        pltpu.make_async_copy(tw, twv, local_sem.at[2]),
        pltpu.make_async_copy(haar, haarv, local_sem.at[3]),
        pltpu.make_async_copy(hw, hwv, local_sem.at[4]),
        pltpu.make_async_copy(qw, qwv, local_sem.at[5]),
        pltpu.make_async_copy(kw, kwv, local_sem.at[6]),
        pltpu.make_async_copy(heads, headsv, local_sem.at[7]),
    ]
    for copy in local:
        copy.start()

    barrier = pltpu.get_barrier_semaphore()
    for d in range(1, nh):
        pl.semaphore_signal(barrier, inc=1, device_id={"height": lax.rem(h + d, nh)}, device_id_type=MESH)
    for d in range(1, nt):
        pl.semaphore_signal(barrier, inc=1, device_id={"tm": lax.rem(t + d, nt)}, device_id_type=MESH)

    total = frames + 2
    for edge, slot in ((0, 0), (nh - 1, rows + 1)):
        @pl.when(h == edge)
        def _():
            vid[:, slot] = jnp.zeros((total, cols, chan), bf16)

    @pl.when(t == 0)
    def _():
        for f in range(2):
            vid[f] = jnp.zeros((rows + 2, cols, chan), bf16)

    for d in range(1, nt):
        @pl.when(t < d)
        def _():
            gl[d] = jnp.zeros(gl.shape[1:], bf16)

    pl.semaphore_wait(barrier, nh - 1 + nt - 1)

    later = {"tm": lax.rem(t + 1, nt)}
    above, below = {"height": lax.rem(h + nh - 1, nh)}, {"height": lax.rem(h + 1, nh)}
    tail = video.at[pl.ds(frames - 2, 2)]
    mine = pl.ds(2, frames)
    halo = [
        remote(video.at[:, 0], vid.at[mine, rows + 1], hsend.at[0], hrecv.at[0], **above),
        remote(video.at[:, rows - 1], vid.at[mine, 0], hsend.at[1], hrecv.at[1], **below),
    ]
    past = [
        remote(tail.at[:, 0], vid.at[pl.ds(0, 2), 1], vsend.at[0], vrecv.at[0], **later),
        remote(tail.at[:, rows - 1], vid.at[pl.ds(0, 2), rows], vsend.at[1], vrecv.at[1], **later),
        remote(
            tail.at[:, pl.ds(1, rows - 2)], vid.at[pl.ds(0, 2), pl.ds(2, rows - 2)],
            vsend.at[2], vrecv.at[2], **later,
        ),
    ]
    relay = [
        remote(vid.at[pl.ds(0, 2), 1], vid.at[pl.ds(0, 2), rows + 1], gsend.at[0], grecv.at[0], **above),
        remote(vid.at[pl.ds(0, 2), rows], vid.at[pl.ds(0, 2), 0], gsend.at[1], grecv.at[1], **below),
    ]
    up, down, has_past, has_next = h > 0, h < nh - 1, t > 0, t < nt - 1
    sends = (up, down)
    receives = (down, up)

    weights, onward = {}, {}
    for a in range(3):
        piece = wfull.at[a, :, own_in, :]
        weights[0, a] = remote(
            sw.at[a], piece, wsend.at[0, a], wrecv.at[0, a], height=sibling
        )
        for d in range(1, chips):
            weights[d, a] = remote(
                sw.at[a], piece, wsend.at[d, a], wrecv.at[d, a],
                height=lax.rem(chip + d, chips) * 2 + core,
            )
            origin = lax.rem(chip + chips - d, chips) * 2 + core
            held = wfull.at[a, :, pl.ds(pl.multiple_of(origin * cin, cin), cin), :]
            onward[d, a] = remote(held, held, fsend.at[d, a], frecv.at[d, a], height=sibling)

    for a in range(3):
        for d in range(1, chips):
            weights[d, a].start()
        weights[0, a].start()
    for cond, copy in zip(sends, halo):
        pl.when(cond)(copy.start)
    for copy in past:
        pl.when(has_next)(copy.start)

    column = lax.broadcasted_iota(jnp.int32, (cols, chan), 0)
    scale = gain[...]

    def activate(f, r):
        values = vid[f, r].astype(f32)
        square = jnp.mean(values * values, axis=-1, keepdims=True)
        normed = values * lax.rsqrt(square + epsilon) * scale
        acted = normed * jax.nn.sigmoid(normed)
        before = jnp.where(column == 0, 0.0, pltpu.roll(acted, 1, 0))
        after = jnp.where(column == cols - 1, 0.0, pltpu.roll(acted, cols - 1, 0))
        patches[f, r, :, pl.ds(0, chan)] = before.astype(bf16)
        patches[f, r, :, pl.ds(chan, chan)] = acted.astype(bf16)
        patches[f, r, :, pl.ds(2 * chan, chan)] = after.astype(bf16)

    def activate_rows(first, count, row, height):
        def step(i, carry):
            activate(first + lax.div(i, height), row + lax.rem(i, height))
            return carry
        lax.fori_loop(0, count * height, step, 0)

    def receive(copies):
        for copy in copies:
            copy.wait_recv()

    local[0].wait()
    activate_rows(2, frames, 1, rows)
    for i in range(2):
        pl.when(has_past)(past[i].wait_recv)
        pl.when(has_past & sends[i])(relay[i].start)
    for i, row in ((0, rows + 1), (1, 0)):
        pl.when(receives[i])(halo[i].wait_recv)
        activate_rows(2, frames, row, 1)
    for d in range(1, chips):
        weights[d, 0].wait_recv()
        onward[d, 0].start()
    for d in range(1, chips):
        weights[d, 1].wait_recv()
        onward[d, 1].start()
    pl.when(has_past)(past[2].wait_recv)
    activate_rows(0, 2, 1, rows)
    for i, row in ((0, rows + 1), (1, 0)):
        pl.when(has_past & receives[i])(relay[i].wait_recv)
        activate_rows(0, 2, row, 1)
    local[1].wait()
    for a in range(3):
        if a == 1:
            for d in range(1, chips):
                weights[d, 2].wait_recv()
                onward[d, 2].start()
        weights[0, a].wait_recv()
        receive([onward[d, a] for d in range(1, chips)])
        taps = wfull[a].reshape(3 * chan, wfull.shape[3])
        for f in range(total):
            part = jnp.dot(
                patches[f, a : a + rows].reshape(rows * cols, 3 * chan), taps,
                preferred_element_type=f32,
            )
            if a == 0:
                acc[f] = part
            elif a == 1:
                acc[f] += part
            else:
                sp[f] = (acc[f] + part).astype(bf16)

    local[2].wait()
    for f in range(frames):
        temporal = jnp.dot(sp[f], twv[0], preferred_element_type=f32)
        for k in (1, 2):
            temporal += jnp.dot(sp[f + k], twv[k], preferred_element_type=f32)
        own = vid[f + 2, 1 : rows + 1].reshape(rows * cols, chan).astype(f32)
        mg[f] = (own + temporal).astype(bf16)

    local[3].wait()
    half = cols // 2
    for j in range(rows // 2):
        pair = pl.ds(2 * j * cols, 2 * cols)
        block = jnp.concatenate([mg[0, pair], mg[1, pair]], axis=0)
        split = jnp.dot(haarv[...], block, preferred_element_type=f32) * (inv_root * inv_root * inv_root)
        for band in range(8):
            bands[pl.ds(j * half, half), pl.ds(band * chan, chan)] = split[
                band * half : (band + 1) * half
            ].astype(bf16)
    local[4].wait()
    latent = jnp.dot(bands[...], hwv[...], preferred_element_type=f32).astype(bf16)
    gl[0] = latent

    shares = [None]
    for d in range(1, nt):
        shares.append(
            remote(gl.at[0], gl.at[d], lsend.at[d], lrecv.at[d], tm=lax.rem(t + d, nt))
        )
    for d in range(1, nt):
        pl.when(t + d < nt)(shares[d].start)

    local[5].wait()
    local[6].wait()
    local[7].wait()
    queries = jnp.dot(latent, qwv[...], preferred_element_type=f32).astype(bf16).astype(f32)
    width = latent.shape[1]
    group = headsv.shape[0]
    for d in range(nt):
        if d:
            pl.when(t >= d)(shares[d].wait_recv)
        keys = jnp.dot(gl[d], kwv[...], preferred_element_type=f32).astype(bf16).astype(f32)
        product = queries * keys
        high = product.astype(bf16)
        low = (product - high.astype(f32)).astype(bf16)
        for c in range(width // group):
            part = slice(c * group, (c + 1) * group)
            score = jnp.dot(high[:, part], headsv[...], preferred_element_type=f32)
            score += jnp.dot(low[:, part], headsv[...], preferred_element_type=f32)
            score = score * HEAD_DIM ** (-0.5)
            sc[d, :, part] = score if d == 0 else jnp.where(t >= d, score, -1e30)
    top = sc[0]
    for d in range(1, nt):
        top = jnp.maximum(top, sc[d])
    denominator = jnp.zeros_like(top)
    for d in range(nt):
        weight = jnp.exp(sc[d] - top)
        sc[d] = weight
        denominator += weight
    mixed = jnp.zeros_like(top)
    for d in range(nt):
        mixed += (sc[d] / denominator).astype(bf16).astype(f32) * gl[d].astype(f32)
    result = latent.astype(f32) + mixed.astype(bf16).astype(f32)
    out[...] = result.astype(bf16).reshape(out.shape)

    for i in range(2):
        pl.when(sends[i])(halo[i].wait_send)
        pl.when(has_past & sends[i])(relay[i].wait_send)
    for copy in past:
        pl.when(has_next)(copy.wait_send)
    for copy in list(weights.values()) + list(onward.values()):
        copy.wait_send()
    for d in range(1, nt):
        pl.when(t + d < nt)(shares[d].wait_send)


def body(nh, nt, video, norm_gain, sw, tw, hw, qw, kw):
    frames, rows, cols, chan = video.shape
    outward, width = sw.shape[3], hw.shape[1]
    bf16, f32 = jnp.bfloat16, jnp.float32
    group = min(256, width)
    ids = np.arange(group) // HEAD_DIM
    heads = jnp.asarray(ids[:, None] == ids[None, :], bf16)
    haar = jnp.asarray(haar_matrix(cols), bf16)
    total, places = frames + 2, rows // 2 * (cols // 2)
    dma = pltpu.SemaphoreType.DMA
    anywhere, vmem = pl.BlockSpec(memory_space=pltpu.HBM), pl.BlockSpec(memory_space=pltpu.VMEM)
    return pl.pallas_call(
        functools.partial(kernel, nh, nt),
        out_shape=jax.ShapeDtypeStruct((frames // 2, rows // 2, cols // 2, width), bf16),
        in_specs=[anywhere, vmem] + [anywhere] * 7,
        out_specs=vmem,
        scratch_shapes=[
            pltpu.VMEM((total, rows + 2, cols, chan), bf16),
            pltpu.VMEM((3, 3, chan, outward), bf16),
            pltpu.VMEM(tw.shape, bf16),
            pltpu.VMEM(hw.shape, bf16),
            pltpu.VMEM(qw.shape, bf16),
            pltpu.VMEM(kw.shape, bf16),
            pltpu.VMEM(haar.shape, bf16),
            pltpu.VMEM(heads.shape, bf16),
            pltpu.VMEM((total, rows + 2, cols, 3 * chan), bf16),
            pltpu.VMEM((total, rows * cols, outward), f32),
            pltpu.VMEM((total, rows * cols, outward), bf16),
            pltpu.VMEM((frames, rows * cols, chan), bf16),
            pltpu.VMEM((places, 8 * chan), bf16),
            pltpu.VMEM((nt, places, width), bf16),
            pltpu.VMEM((nt, places, width), f32),
            dma((8,)),
            dma((nh // 2, 3)), dma((nh // 2, 3)), dma((nh // 2, 3)), dma((nh // 2, 3)),
            dma((2,)), dma((2,)), dma((2,)), dma((2,)), dma((3,)), dma((3,)),
            dma((nt,)), dma((nt,)),
        ],
        compiler_params=pltpu.CompilerParams(
            collective_id=0, has_side_effects=True, vmem_limit_bytes=60 * 1024 * 1024
        ),
        cost_estimate=pl.CostEstimate(
            flops=2 * 10**9, bytes_accessed=5 * 10**6, transcendentals=10**6
        ),
    )(video, norm_gain.reshape(1, chan), sw, tw, hw, qw, kw, haar, heads)


def solution(mesh):
    in_specs = (
        P(("groups", "tm"), "height", None, None),
        P(),
        P(None, None, "height", None),
        P(),
        P(),
        P(),
        P(),
    )
    out_specs = P(("groups", "tm"), "height", None, None)
    run = functools.partial(body, mesh.shape["height"], mesh.shape["tm"])
    return jax.shard_map(run, mesh=mesh, in_specs=in_specs, out_specs=out_specs, check_vma=False)
```
